256 devices in a mesh: pairs: 32 (over z, x), side: 2 (over core), mp: 4 (over y).
Axes of the slice: x: 4, y: 4, z: 8, core: 2. Of those that a mesh axis runs over, the one named last changes fastest.
Arguments:
- enc_tokens: bfloat16 [256, 512, 1024], P('pairs', 'mp'), may hold values from -6 to 6
- pair_views: int32 [128, 2], replicated, may hold values from 0 to 255, as said below
- embed_weight: bfloat16 [1024, 768], replicated, may hold values from -0.1875 to 0.1875
- self_qkv: bfloat16 [2, 3, 768, 768], P('side', None, None, 'mp'), may hold values from -10 to 10
- self_out: bfloat16 [2, 768, 768], P('side'), may hold values from -0.21875 to 0.21875
- cross_query: bfloat16 [2, 768, 768], P('side', None, 'mp'), may hold values from -1 to 1
- cross_kv: bfloat16 [2, 2, 768, 768], P('side', None, None, 'mp'), may hold values from -10 to 10
- cross_out: bfloat16 [2, 768, 768], P('side'), may hold values from -0.21875 to 0.21875
- norm_gains: float32 [2, 4, 768], P('side'), may hold values from 0.25 to 1.75
- head_weight: bfloat16 [2, 768, 1024], P('side'), may hold values from -0.21875 to 0.21875
Outputs:
- pointmaps: bfloat16 [128, 2, 512, 1024], P('pairs', 'side', 'mp')
The draws below stay inside these ranges and needn't reach their ends.
Inputs may be any that keep to these rules, and one draw needn't show every extreme that they name: `pair_views`: the two ids of a pair lie in different blocks of 8 consecutive ids. For each block of 4 consecutive pairs and each side, at most 1 of its ids lie in any one block of 8 consecutive ids, and some block holds exactly 1.
All inputs are finite; a program needn't handle non-finite values.
Results may differ from the reference program's by a relative error of at most 0.023.
Values may be sent and summed in bfloat16 or wider, within the bound.
No kernel may reach another device: no remote copies, remote signals or barrier semaphores. Data moves between devices by JAX's collectives and lax.ppermute only.
A program may use at most 128 MiB of HBM per device.

```python
import jax
import jax.numpy as jnp
from jax import lax

D = 768
HEADS = 12
ENC = 1024
PATCH_OUT = 1024
TOK = 512
PAIR_DEV = 4
VIEW_DEV = 8
PAIRS = 128
VIEWS = 256


def draw_pair_views(key, part):
    key = jax.random.fold_in(key, 7)
    owners = VIEWS // VIEW_DEV
    groups = PAIRS // PAIR_DEV
    capacity = (PAIR_DEV + owners - 1) // owners
    subkeys = jax.random.split(key, 4)
    orders = jax.vmap(lambda single: jax.random.permutation(single, owners))(jax.random.split(subkeys[0], groups))
    slot_owner = orders[:, jnp.arange(PAIR_DEV) // capacity]
    offset = jax.random.randint(subkeys[1], (groups, 1), 1, owners)
    other_owner = (slot_owner + offset) % owners
    first_view = slot_owner * VIEW_DEV + jax.random.randint(subkeys[2], (groups, PAIR_DEV), 0, VIEW_DEV)
    second = other_owner * VIEW_DEV + jax.random.randint(subkeys[3], (groups, PAIR_DEV), 0, VIEW_DEV)
    return jnp.stack([first_view.reshape(-1), second.reshape(-1)], axis=1).astype(jnp.int32)


def draw_enc_tokens(key, part):
    key = jax.random.fold_in(key, 3)
    noise = jnp.clip(jax.random.normal(key, (VIEWS, TOK, ENC), jnp.float32), -6.0, 6.0)
    return noise.astype(jnp.bfloat16)


def scaled_normal(key, shape):
    return jnp.clip(jax.random.normal(key, shape, jnp.float32), -6.0, 6.0) * D ** (-0.5)


def draw_self_qkv(key, part):
    key = jax.random.fold_in(key, 5)
    base = scaled_normal(key, (2, 3, D, D))
    return base.astype(jnp.bfloat16)


def cross_base(key):
    return scaled_normal(key, (2, 3, D, D))


def draw_cross_query(key, part):
    base = cross_base(key)
    return base[:, 0].astype(jnp.bfloat16)


def draw_cross_kv(key, part):
    base = cross_base(key)
    key_part = base[:, 1]
    return jnp.stack([key_part, base[:, 2]], axis=1).astype(jnp.bfloat16)


def levels(key, dims, shards, low, high):
    level = 1.0
    for position, parts in shards:
        steps = jax.random.uniform(jax.random.fold_in(jax.random.fold_in(key, 6), position), (parts,), jnp.float32, low / len(shards), high / len(shards))
        level = level * jnp.repeat(jnp.exp(steps), dims[position] // parts).reshape((-1,) + (1,) * (len(dims) - 1 - position))
    return level


def scatter_about(own_key, shape, deviation, most, pieces=(), dtype=jnp.bfloat16):
    drawn = deviation * jax.random.normal(own_key, shape, jnp.float32)
    if pieces:
        drawn = drawn * levels(own_key, shape, pieces, -0.22, 0.18)
    return jnp.clip(drawn, -most, most).astype(dtype)


def setup_inputs(seed: int = 0) -> dict:
    splits = jax.random.split(jax.random.key(seed), 11)
    return {
        "enc_tokens": draw_enc_tokens(jax.random.fold_in(splits[10], 71), 0),
        "pair_views": draw_pair_views(jax.random.fold_in(splits[10], 71), 0),
        "embed_weight": scatter_about(splits[2], (ENC, D), ENC ** -0.5, 0.1875),
        "self_qkv": draw_self_qkv(jax.random.fold_in(splits[10], 71), 0),
        "self_out": scatter_about(splits[4], (2, D, D), D ** -0.5, 0.21875, ((0, 2),)),
        "cross_query": draw_cross_query(jax.random.fold_in(splits[10], 71), 0),
        "cross_kv": draw_cross_kv(jax.random.fold_in(splits[10], 71), 0),
        "cross_out": scatter_about(splits[7], (2, D, D), D ** -0.5, 0.21875, ((0, 2),)),
        "norm_gains": jnp.clip(1.0 + 0.15 * jax.random.normal(splits[8], (2, 4, D), jnp.float32), 0.25, 1.75),
        "head_weight": scatter_about(splits[9], (2, D, PATCH_OUT), D ** -0.5, 0.21875, ((0, 2),)),
    }


def layer_norm(values, gain):
    average = lax.optimization_barrier(jnp.mean(values, axis=-1, keepdims=True))
    centred = values - average
    spread = lax.optimization_barrier(jnp.mean(centred * centred, axis=-1, keepdims=True))
    return centred * lax.rsqrt(spread + 1e-06) * gain

def attend(queries, key_rows, value_rows):
    token_count = queries.shape[0]
    shaped = (token_count, HEADS, D // HEADS)
    query_heads = queries.reshape(shaped).astype(jnp.float32)
    key_heads = key_rows.reshape(shaped).astype(jnp.float32)
    value_heads = value_rows.reshape(shaped).astype(jnp.float32)
    scores = jnp.einsum('qhd,khd->hqk', query_heads, key_heads) * (D // HEADS) ** (-0.5)
    weights = jax.nn.softmax(scores, axis=-1).astype(jnp.bfloat16)
    mixture = jnp.einsum('hqk,khd->qhd', weights.astype(jnp.float32), value_heads)
    return mixture.reshape(token_count, D).astype(jnp.bfloat16)

def decode_side(own_rows, partner_rows, gain_rows, qkv_weight, out_weight, query_weight, kv_weight, cross_weight, head_proj):
    normed = layer_norm(own_rows.astype(jnp.float32), gain_rows[0]).astype(jnp.bfloat16)
    projected = jnp.einsum('td,cde->cte', normed.astype(jnp.float32), qkv_weight.astype(jnp.float32)).astype(jnp.bfloat16)
    attended = attend(projected[0], projected[1], projected[2])
    after_self = own_rows.astype(jnp.float32) + jnp.dot(attended, out_weight, preferred_element_type=jnp.float32)
    partner_normed = layer_norm(partner_rows.astype(jnp.float32), gain_rows[2]).astype(jnp.bfloat16)
    partner_kv = jnp.einsum('td,cde->cte', partner_normed.astype(jnp.float32), kv_weight.astype(jnp.float32)).astype(jnp.bfloat16)
    query_normed = layer_norm(after_self, gain_rows[1]).astype(jnp.bfloat16)
    cross_queries = jnp.dot(query_normed, query_weight, preferred_element_type=jnp.float32).astype(jnp.bfloat16)
    crossed = attend(cross_queries, partner_kv[0], partner_kv[1])
    after_cross = after_self + jnp.dot(crossed, cross_weight, preferred_element_type=jnp.float32)
    final_rows = layer_norm(after_cross, gain_rows[3]).astype(jnp.bfloat16)
    return jnp.dot(final_rows, head_proj, preferred_element_type=jnp.float32).astype(jnp.bfloat16)

def reference(enc_tokens, pair_views, embed_weight, self_qkv, self_out, cross_query, cross_kv, cross_out, norm_gains, head_weight):
    embedded = jnp.dot(enc_tokens.reshape(VIEWS * TOK, ENC), embed_weight, preferred_element_type=jnp.float32)
    embedded = embedded.astype(jnp.bfloat16).reshape(VIEWS, TOK, D)

    def one_pair(view_pair):
        first_view = embedded[view_pair[0]]
        second_view = embedded[view_pair[1]]
        left_side = decode_side(first_view, second_view, norm_gains[0], self_qkv[0], self_out[0], cross_query[0], cross_kv[0], cross_out[0], head_weight[0])
        right_side = decode_side(second_view, first_view, norm_gains[1], self_qkv[1], self_out[1], cross_query[1], cross_kv[1], cross_out[1], head_weight[1])
        return jnp.stack([left_side, right_side])
    return lax.map(one_pair, pair_views)
```

```python
import jax
import jax.numpy as jnp
from jax import lax
from jax.experimental import pallas as pl
from jax.experimental.pallas import tpu as pltpu
from jax.sharding import PartitionSpec as P

D = 768
HEADS = 12
HEAD_DIM = D // HEADS
TOK = 512
MP = 4
COLS = D // MP
WINDOW = 256
KINDS = 3
PIECE_ROWS = 8
PIECE_COLS = 384
HALVES = D // PIECE_COLS
LOG_SCALE = 1.4426950408889634 * HEAD_DIM**-0.5
VMEM = 48 * 2**20
MOST_VMEM = 61 * 2**20


def layer_norm(values, gain):
    average = jnp.mean(values, axis=-1, keepdims=True)
    centred = values - average
    spread = jnp.mean(centred * centred, axis=-1, keepdims=True)
    return centred * lax.rsqrt(spread + 1e-06) * gain


def estimate(flops, moved, exps=0):
    return pl.CostEstimate(flops=int(flops), bytes_accessed=int(moved), transcendentals=int(exps))


def embed_kernel(side_ref, tokens_ref, weight_ref, out_ref, held_ref, held_weight_ref, sems):
    views, rows, width = held_ref.shape
    fetched = pltpu.make_async_copy(tokens_ref.at[pl.ds(side_ref[0] * views, views)], held_ref, sems.at[0])
    fetched.start()
    halves = []
    for half in range(HALVES):
        columns = slice(half * PIECE_COLS, (half + 1) * PIECE_COLS)
        halves.append(
            pltpu.make_async_copy(weight_ref.at[:, columns], held_weight_ref.at[:, columns], sems.at[1 + half])
        )
        halves[half].start()
    fetched.wait()
    tokens = held_ref[...].reshape(views * rows, width)
    for half in range(HALVES):
        halves[half].wait()
        columns = slice(half * PIECE_COLS, (half + 1) * PIECE_COLS)
        embedded = jnp.dot(tokens, held_weight_ref[:, columns], preferred_element_type=jnp.float32)
        for view in range(views):
            for block in range(rows // PIECE_ROWS):
                top = view * rows + block * PIECE_ROWS
                out_ref[block * HALVES + half, view] = embedded[top : top + PIECE_ROWS].astype(jnp.bfloat16)


def embed(enc_tokens, embed_weight, side_index):
    views, rows, width = enc_tokens.shape
    taken = views // 2
    pieces = rows // PIECE_ROWS * HALVES
    return pl.pallas_call(
        embed_kernel,
        out_shape=jax.ShapeDtypeStruct((pieces, taken, PIECE_ROWS, PIECE_COLS), jnp.bfloat16),
        in_specs=[pl.BlockSpec(memory_space=pltpu.SMEM)] + [pl.BlockSpec(memory_space=pltpu.HBM)] * 2,
        out_specs=pl.BlockSpec(memory_space=pltpu.VMEM),
        scratch_shapes=[
            pltpu.VMEM((taken, rows, width), jnp.bfloat16),
            pltpu.VMEM((width, D), jnp.bfloat16),
            pltpu.SemaphoreType.DMA((1 + HALVES,)),
        ],
        compiler_params=pltpu.CompilerParams(vmem_limit_bytes=MOST_VMEM),
        cost_estimate=estimate(2 * taken * rows * width * D, 2 * (taken * rows * (width + D) + width * D)),
        name="embed",
    )(side_index.reshape(1), enc_tokens, embed_weight)


def pick_kernel(slots_ref, own_ref, other_ref, out_ref):
    count = own_ref.shape[0]

    def step(pair, carry):
        code = slots_ref[pair]
        foreign = code >= count
        slot = jnp.where(foreign, code - count, code)
        out_ref[pair] = jnp.where(foreign, other_ref[slot], own_ref[slot])
        return carry

    lax.fori_loop(0, out_ref.shape[0], step, 0, unroll=8)


def pick(slots, own, other):
    shape = (slots.shape[0],) + own.shape[1:]
    return pl.pallas_call(
        pick_kernel,
        out_shape=jax.ShapeDtypeStruct(shape, own.dtype),
        in_specs=[
            pl.BlockSpec(memory_space=pltpu.SMEM),
            pl.BlockSpec(memory_space=pltpu.VMEM),
            pl.BlockSpec(memory_space=pltpu.VMEM),
        ],
        out_specs=pl.BlockSpec(memory_space=pltpu.VMEM),
        compiler_params=pltpu.CompilerParams(vmem_limit_bytes=VMEM),
        cost_estimate=estimate(own.size, 6 * own.size),
        name="pick",
    )(slots, own, other)


def unpack(pieces_ref, rows_ref):
    per_device = TOK // MP
    for piece in range(pieces_ref.shape[0]):
        source, owner = divmod(piece, MP)
        block, half = divmod(source, HALVES)
        top = owner * per_device + block * PIECE_ROWS
        rows_ref[top : top + PIECE_ROWS, half * PIECE_COLS : (half + 1) * PIECE_COLS] = pieces_ref[
            piece
        ].astype(jnp.float32)


def normalise(rows_ref, gain, out_ref):
    for top in range(0, TOK, 128):
        out_ref[top : top + 128] = layer_norm(rows_ref[top : top + 128], gain).astype(jnp.bfloat16)


def project(rows, weight_ref, kind, quad):
    parts = []
    column = quad * WINDOW
    while column < (quad + 1) * WINDOW:
        owner, first = divmod(column, COLS)
        last = min(COLS, first + (quad + 1) * WINDOW - column)
        parts.append(weight_ref[owner, kind, first:last])
        column += last - first
    return lax.dot_general(
        rows, jnp.concatenate(parts, axis=0), (((1,), (1,)), ((), ())), preferred_element_type=jnp.float32
    )


def attend(queries, keys, values):
    lane = lax.broadcasted_iota(jnp.int32, (1, WINDOW), 1)
    keys = keys.astype(jnp.bfloat16)
    values = values.astype(jnp.bfloat16)
    attended = jnp.zeros(queries.shape, jnp.float32)
    for head in range(WINDOW // HEAD_DIM):
        inside = lane // HEAD_DIM == head
        masked = jnp.where(inside, queries, 0.0).astype(jnp.bfloat16)
        scores = lax.dot_general(
            masked, keys, (((1,), (1,)), ((), ())), preferred_element_type=jnp.float32
        )
        scores = scores * LOG_SCALE
        weights = jnp.exp2(scores - jnp.max(scores, axis=-1, keepdims=True))
        total = jnp.sum(weights, axis=-1, keepdims=True)
        mixture = jnp.dot(weights.astype(jnp.bfloat16), values, preferred_element_type=jnp.float32)
        attended = jnp.where(inside, mixture * (1.0 / total), attended)
    return attended.astype(jnp.bfloat16)


def self_kernel(
    pieces_ref, gathered_ref, out_weight_ref, gain_ref, out_ref, normed_ref, attended_ref, weight_ref, sem
):
    fetched = pltpu.make_async_copy(gathered_ref.at[:, 0:KINDS], weight_ref, sem)
    fetched.start()
    unpack(pieces_ref, out_ref)
    normalise(out_ref, gain_ref[0:1], normed_ref)
    normed = normed_ref[...]
    fetched.wait()
    for quad in range(D // WINDOW):
        attended_ref[:, quad * WINDOW : (quad + 1) * WINDOW] = attend(
            *(project(normed, weight_ref, kind, quad) for kind in range(KINDS))
        )
    out_ref[...] += jnp.dot(attended_ref[...], out_weight_ref[...], preferred_element_type=jnp.float32)


def cross_kernel(
    after_ref,
    pieces_ref,
    gathered_ref,
    out_weight_ref,
    gain_ref,
    out_ref,
    rows_ref,
    query_ref,
    partner_ref,
    attended_ref,
    weight_ref,
    sem,
):
    fetched = pltpu.make_async_copy(gathered_ref.at[:, KINDS : 2 * KINDS], weight_ref, sem)
    fetched.start()
    unpack(pieces_ref, rows_ref)
    normalise(rows_ref, gain_ref[2:3], partner_ref)
    normalise(after_ref, gain_ref[1:2], query_ref)
    queries, partner = query_ref[...], partner_ref[...]
    fetched.wait()
    for quad in range(D // WINDOW):
        attended_ref[:, quad * WINDOW : (quad + 1) * WINDOW] = attend(
            project(queries, weight_ref, 0, quad),
            project(partner, weight_ref, 1, quad),
            project(partner, weight_ref, 2, quad),
        )
    rows_ref[...] = after_ref[...] + jnp.dot(
        attended_ref[...], out_weight_ref[...], preferred_element_type=jnp.float32
    )
    normalise(rows_ref, gain_ref[3:4], out_ref)


def in_vmem(count):
    return [pl.BlockSpec(memory_space=pltpu.VMEM)] * count


def in_hbm(count):
    return [pl.BlockSpec(memory_space=pltpu.HBM)] * count


def fetched_weights():
    return [pltpu.VMEM((MP, KINDS, COLS, D), jnp.bfloat16), pltpu.SemaphoreType.DMA]


def self_block(pieces, weights, out_weight, gains):
    return pl.pallas_call(
        self_kernel,
        out_shape=jax.ShapeDtypeStruct((TOK, D), jnp.float32),
        in_specs=in_vmem(1) + [pl.BlockSpec(memory_space=pltpu.HBM)] + in_vmem(2),
        out_specs=in_vmem(1)[0],
        scratch_shapes=[pltpu.VMEM((TOK, D), jnp.bfloat16)] * 2 + fetched_weights(),
        compiler_params=pltpu.CompilerParams(vmem_limit_bytes=VMEM),
        cost_estimate=estimate(8 * TOK * D * D + 4 * TOK * TOK * D, 8 * 2**20, HEADS * TOK * TOK),
        name="self_block",
    )(pieces, weights, out_weight, gains)


def cross_block(after_self, pieces, weights, out_weight, gains):
    return pl.pallas_call(
        cross_kernel,
        out_shape=jax.ShapeDtypeStruct((TOK, D), jnp.bfloat16),
        in_specs=in_vmem(2) + [pl.BlockSpec(memory_space=pltpu.HBM)] + in_vmem(2),
        out_specs=in_vmem(1)[0],
        scratch_shapes=[pltpu.VMEM((TOK, D), jnp.float32)] + [pltpu.VMEM((TOK, D), jnp.bfloat16)] * 3 + fetched_weights(),
        compiler_params=pltpu.CompilerParams(vmem_limit_bytes=VMEM),
        cost_estimate=estimate(8 * TOK * D * D + 4 * TOK * TOK * D, 8 * 2**20, HEADS * TOK * TOK),
        name="cross_block",
    )(after_self, pieces, weights, out_weight, gains)


def together_kernel(*refs):
    *sources, out_ref, held_ref, in_sems, out_sems = refs
    arriving = []
    for source in sources:
        for kind in range(source.shape[0]):
            place = len(arriving)
            arriving.append(pltpu.make_async_copy(source.at[kind], held_ref.at[place], in_sems.at[place]))
            arriving[place].start()
    leaving = []
    for place, copy in enumerate(arriving):
        copy.wait()
        leaving.append(pltpu.make_async_copy(held_ref.at[place], out_ref.at[place], out_sems.at[place]))
        leaving[place].start()
    for copy in leaving:
        copy.wait()


def together(*weights):
    count = sum(weight.shape[0] for weight in weights)
    shape = (count,) + weights[0].shape[1:]
    return pl.pallas_call(
        together_kernel,
        out_shape=jax.ShapeDtypeStruct(shape, jnp.bfloat16),
        in_specs=in_hbm(len(weights)),
        out_specs=in_hbm(1)[0],
        scratch_shapes=[
            pltpu.VMEM(shape, jnp.bfloat16),
            pltpu.SemaphoreType.DMA((count,)),
            pltpu.SemaphoreType.DMA((count,)),
        ],
        compiler_params=pltpu.CompilerParams(vmem_limit_bytes=MOST_VMEM),
        cost_estimate=estimate(0, 4 * count * COLS * D),
        name="together",
    )(*weights)


def local(
    enc_tokens,
    pair_views,
    embed_weight,
    self_qkv,
    self_out,
    cross_query,
    cross_kv,
    cross_out,
    norm_gains,
    head_weight,
):
    side_index = lax.axis_index("side")
    flip = [(0, 1), (1, 0)]
    weights = together(*(jnp.swapaxes(weight, 1, 2) for weight in (self_qkv[0], cross_query, cross_kv[0])))
    weights = lax.all_gather(weights, "mp", axis=0)
    spread = lax.all_to_all(
        embed(enc_tokens, embed_weight, side_index), "pairs", split_axis=0, concat_axis=0, tiled=True
    )
    views = enc_tokens.shape[0]
    taken = views // 2
    own = spread.reshape((-1,) + spread.shape[2:])
    other = lax.ppermute(own, "side", flip)
    wanted = jnp.where(side_index == 0, pair_views[:, 0], pair_views[:, 1])
    within = wanted % views
    slots = wanted // views * taken + within % taken
    slots = jnp.where(within // taken == side_index, slots, slots + own.shape[0])
    packets = pick(slots, own, other)
    pieces = lax.all_to_all(packets, ("pairs", "mp"), split_axis=0, concat_axis=0, tiled=True)
    partner = lax.ppermute(pieces, "side", flip)
    after_self = self_block(pieces, weights, self_out[0], norm_gains[0])
    final_rows = cross_block(after_self, partner, weights, cross_out[0], norm_gains[0])
    final_rows = lax.all_to_all(
        final_rows.reshape(MP, TOK // MP, D), "mp", split_axis=0, concat_axis=0, tiled=True
    )
    result = jnp.einsum("prd,de->pre", final_rows, head_weight[0], preferred_element_type=jnp.float32)
    return result.astype(jnp.bfloat16)[:, None]


def solution(mesh):
    placed = (
        P("pairs", "mp", None),
        P(),
        P(),
        P("side", None, None, "mp"),
        P("side", None, None),
        P("side", None, "mp"),
        P("side", None, None, "mp"),
        P("side", None, None),
        P("side", None, None),
        P("side", None, None),
    )
    return jax.shard_map(
        local, mesh=mesh, in_specs=placed, out_specs=P("pairs", "side", "mp", None), check_vma=False
    )
```

```python
import jax
import jax.numpy as jnp
from jax import lax
from jax.experimental import pallas as pl
from jax.experimental.pallas import tpu as pltpu
from jax.sharding import PartitionSpec as P

D = 768
HEADS = 12
HEAD_DIM = D // HEADS
TOK = 512
MP = 4
COLS = D // MP
WINDOW = 256
KINDS = 3
PIECE_ROWS = 8
PIECE_COLS = 384
HALVES = D // PIECE_COLS
APART = (0, -1 % MP, 1, 2)
CHUNK = 512
AHEAD = 1
LOG_SCALE = 1.4426950408889634 * HEAD_DIM**-0.5
VMEM = 48 * 2**20
MOST_VMEM = 61 * 2**20


def layer_norm(values, gain):
    average = jnp.mean(values, axis=-1, keepdims=True)
    centred = values - average
    spread = jnp.mean(centred * centred, axis=-1, keepdims=True)
    return centred * lax.rsqrt(spread + 1e-06) * gain


def estimate(flops, moved, exps=0):
    return pl.CostEstimate(flops=int(flops), bytes_accessed=int(moved), transcendentals=int(exps))


def in_vmem(count):
    return [pl.BlockSpec(memory_space=pltpu.VMEM)] * count


def in_hbm(count):
    return [pl.BlockSpec(memory_space=pltpu.HBM)] * count


def embed_kernel(side_ref, tokens_ref, weight_ref, out_ref, held_ref, held_weight_ref, sems):
    views, rows, width = held_ref.shape
    fetched = pltpu.make_async_copy(tokens_ref.at[pl.ds(side_ref[0] * views, views)], held_ref, sems.at[0])
    fetched.start()
    halves = []
    for half in range(HALVES):
        columns = slice(half * PIECE_COLS, (half + 1) * PIECE_COLS)
        halves.append(
            pltpu.make_async_copy(weight_ref.at[:, columns], held_weight_ref.at[:, columns], sems.at[1 + half])
        )
        halves[half].start()
    fetched.wait()
    tokens = held_ref[...].reshape(views * rows, width)
    for half in range(HALVES):
        halves[half].wait()
        columns = slice(half * PIECE_COLS, (half + 1) * PIECE_COLS)
        embedded = jnp.dot(tokens, held_weight_ref[:, columns], preferred_element_type=jnp.float32)
        for view in range(views):
            for block in range(rows // PIECE_ROWS):
                top = view * rows + block * PIECE_ROWS
                out_ref[block * HALVES + half, view] = embedded[top : top + PIECE_ROWS].astype(jnp.bfloat16)


def embed(enc_tokens, embed_weight, side_index):
    views, rows, width = enc_tokens.shape
    taken = views // 2
    pieces = rows // PIECE_ROWS * HALVES
    return pl.pallas_call(
        embed_kernel,
        out_shape=jax.ShapeDtypeStruct((pieces, taken, PIECE_ROWS, PIECE_COLS), jnp.bfloat16),
        in_specs=[pl.BlockSpec(memory_space=pltpu.SMEM)] + [pl.BlockSpec(memory_space=pltpu.HBM)] * 2,
        out_specs=pl.BlockSpec(memory_space=pltpu.VMEM),
        scratch_shapes=[
            pltpu.VMEM((taken, rows, width), jnp.bfloat16),
            pltpu.VMEM((width, D), jnp.bfloat16),
            pltpu.SemaphoreType.DMA((1 + HALVES,)),
        ],
        compiler_params=pltpu.CompilerParams(vmem_limit_bytes=MOST_VMEM),
        cost_estimate=estimate(2 * taken * rows * width * D, 2 * (taken * rows * (width + D) + width * D)),
        name="embed",
    )(side_index.reshape(1), enc_tokens, embed_weight)


def pick_kernel(slots_ref, own_ref, other_ref, out_ref):
    count = own_ref.shape[0]

    def step(pair, carry):
        code = slots_ref[pair]
        foreign = code >= count
        slot = jnp.where(foreign, code - count, code)
        out_ref[pair] = jnp.where(foreign, other_ref[slot], own_ref[slot])
        return carry

    lax.fori_loop(0, out_ref.shape[0], step, 0, unroll=8)


def pick(slots, own, other):
    shape = (slots.shape[0],) + own.shape[1:]
    return pl.pallas_call(
        pick_kernel,
        out_shape=jax.ShapeDtypeStruct(shape, own.dtype),
        in_specs=[
            pl.BlockSpec(memory_space=pltpu.SMEM),
            pl.BlockSpec(memory_space=pltpu.VMEM),
            pl.BlockSpec(memory_space=pltpu.VMEM),
        ],
        out_specs=pl.BlockSpec(memory_space=pltpu.VMEM),
        compiler_params=pltpu.CompilerParams(vmem_limit_bytes=VMEM),
        cost_estimate=estimate(own.size, 6 * own.size),
        name="pick",
    )(slots, own, other)


def unpack(pieces_ref, rows_ref):
    per_device = TOK // MP
    for piece in range(pieces_ref.shape[0]):
        source, owner = divmod(piece, MP)
        block, half = divmod(source, HALVES)
        top = owner * per_device + block * PIECE_ROWS
        rows_ref[top : top + PIECE_ROWS, half * PIECE_COLS : (half + 1) * PIECE_COLS] = pieces_ref[
            piece
        ].astype(jnp.float32)


def normalise(rows_ref, gain, out_ref):
    for top in range(0, TOK, 128):
        out_ref[top : top + 128] = layer_norm(rows_ref[top : top + 128], gain).astype(jnp.bfloat16)


def project(rows, columns_of, quad):
    parts = []
    column = quad * WINDOW
    while column < (quad + 1) * WINDOW:
        owner, first = divmod(column, COLS)
        last = min(COLS, first + (quad + 1) * WINDOW - column)
        parts.append(columns_of(owner, first, last))
        column += last - first
    return lax.dot_general(
        rows, jnp.concatenate(parts, axis=0), (((1,), (1,)), ((), ())), preferred_element_type=jnp.float32
    )


def of_kind(weight_ref, kind):
    return lambda owner, first, last: weight_ref[owner, kind, first:last]


def scores_of(queries, keys, head, top):
    inside = lax.broadcasted_iota(jnp.int32, (1, WINDOW), 1) // HEAD_DIM == head
    masked = jnp.where(inside, queries[top : top + CHUNK], 0.0).astype(jnp.bfloat16)
    return lax.dot_general(masked, keys, (((1,), (1,)), ((), ())), preferred_element_type=jnp.float32)


def attend(quad_of, attended_ref):
    steps = [
        (quad, head, top)
        for quad in range(D // WINDOW)
        for head in range(WINDOW // HEAD_DIM)
        for top in range(0, TOK, CHUNK)
    ]
    lane = lax.broadcasted_iota(jnp.int32, (1, WINDOW), 1)
    held = {}
    sums = {}

    def start(step):
        quad, head, top = step
        if quad not in held:
            queries, keys, values = quad_of(quad)
            held[quad] = (queries * LOG_SCALE, keys.astype(jnp.bfloat16), values.astype(jnp.bfloat16))
        return scores_of(held[quad][0], held[quad][1], head, top)

    ahead = [start(step) for step in steps[:AHEAD]]
    for count, (quad, head, top) in enumerate(steps):
        if count + AHEAD < len(steps):
            ahead.append(start(steps[count + AHEAD]))
        scores = ahead.pop(0)
        weights = jnp.exp2(scores - jnp.max(scores, axis=-1, keepdims=True))
        total = jnp.sum(weights, axis=-1, keepdims=True)
        mixture = jnp.dot(weights.astype(jnp.bfloat16), held[quad][2], preferred_element_type=jnp.float32)
        mixture = mixture * (1.0 / total)
        if head:
            mixture = jnp.where(lane // HEAD_DIM == head, mixture, sums[quad, top])
        sums[quad, top] = mixture
        if head == WINDOW // HEAD_DIM - 1:
            attended_ref[top : top + CHUNK, quad * WINDOW : (quad + 1) * WINDOW] = mixture.astype(jnp.bfloat16)


def self_kernel(
    pieces_ref, gathered_ref, out_weight_ref, gain_ref, out_ref, cross_ref, normed_ref, attended_ref, weight_ref, sems
):
    fetched = []
    for owner in range(MP):
        fetched.append(
            pltpu.make_async_copy(gathered_ref.at[owner, 0:KINDS], weight_ref.at[owner], sems.at[owner])
        )
        fetched[owner].start()
    passed = pltpu.make_async_copy(gathered_ref.at[:, KINDS:], cross_ref, sems.at[MP])
    passed.start()
    unpack(pieces_ref, out_ref)
    normalise(out_ref, gain_ref[0:1], normed_ref)
    normed = normed_ref[...]
    waited = []

    def quad_of(quad):
        while len(waited) <= (quad * WINDOW + WINDOW - 1) // COLS:
            fetched[len(waited)].wait()
            waited.append(True)
        return [project(normed, of_kind(weight_ref, kind), quad) for kind in range(KINDS)]

    attend(quad_of, attended_ref)
    out_ref[...] += jnp.dot(attended_ref[...], out_weight_ref[...], preferred_element_type=jnp.float32)
    passed.wait()


def cross_kernel(
    place_ref, after_ref, pieces_ref, slices0_ref, slices1_ref, slices2_ref, slices3_ref, weight_ref, out_weight_ref,
    gain_ref, out_ref, rows_ref, query_ref, partner_ref, attended_ref, slices_ref, sems,
):
    fetched = []
    for count, source in enumerate((slices0_ref, slices1_ref, slices2_ref, slices3_ref)):
        along_x = lax.rem(place_ref[1] + APART[count], MP)
        for place in range(MP):
            owner = lax.rem(place_ref[0] + APART[place], MP)
            sem = sems.at[count * MP + place]
            fetched.append(pltpu.make_async_copy(source.at[place], slices_ref.at[owner, along_x], sem))
            fetched[-1].start()
    unpack(pieces_ref, rows_ref)
    normalise(rows_ref, gain_ref[2:3], partner_ref)
    normalise(after_ref, gain_ref[1:2], query_ref)
    queries, partner = query_ref[...], partner_ref[...]
    for copy in fetched:
        copy.wait()

    def query_columns(owner, first, last):
        return slices_ref[owner].reshape(COLS, D)[first:last]

    attend(
        lambda quad: (
            project(queries, query_columns, quad),
            project(partner, of_kind(weight_ref, 0), quad),
            project(partner, of_kind(weight_ref, 1), quad),
        ),
        attended_ref,
    )
    rows_ref[...] = after_ref[...] + jnp.dot(
        attended_ref[...], out_weight_ref[...], preferred_element_type=jnp.float32
    )
    normalise(rows_ref, gain_ref[3:4], out_ref)


def self_block(pieces, weights, out_weight, gains):
    rest = weights.shape[1] - KINDS
    return pl.pallas_call(
        self_kernel,
        out_shape=(
            jax.ShapeDtypeStruct((TOK, D), jnp.float32),
            jax.ShapeDtypeStruct((MP, rest, COLS, D), jnp.bfloat16),
        ),
        in_specs=in_vmem(1) + in_hbm(1) + in_vmem(2),
        out_specs=tuple(in_vmem(2)),
        scratch_shapes=[pltpu.VMEM((TOK, D), jnp.bfloat16)] * 2
        + [pltpu.VMEM((MP, KINDS, COLS, D), jnp.bfloat16), pltpu.SemaphoreType.DMA((MP + 1,))],
        compiler_params=pltpu.CompilerParams(vmem_limit_bytes=VMEM),
        cost_estimate=estimate(8 * TOK * D * D + 4 * TOK * TOK * D, 8 * 2**20, HEADS * TOK * TOK),
        name="self_block",
    )(pieces, weights, out_weight, gains)


def cross_block(place, after_self, pieces, slices, weights, out_weight, gains):
    return pl.pallas_call(
        cross_kernel,
        out_shape=jax.ShapeDtypeStruct((TOK, D), jnp.bfloat16),
        in_specs=[pl.BlockSpec(memory_space=pltpu.SMEM)] + in_vmem(2) + in_hbm(MP) + in_vmem(3),
        out_specs=in_vmem(1)[0],
        scratch_shapes=[pltpu.VMEM((TOK, D), jnp.float32)]
        + [pltpu.VMEM((TOK, D), jnp.bfloat16)] * 3
        + [pltpu.VMEM((MP,) + slices[0].shape, jnp.bfloat16), pltpu.SemaphoreType.DMA((MP * MP,))],
        compiler_params=pltpu.CompilerParams(vmem_limit_bytes=VMEM),
        cost_estimate=estimate(8 * TOK * D * D + 4 * TOK * TOK * D, 8 * 2**20, HEADS * TOK * TOK),
        name="cross_block",
    )(place, after_self, pieces, *slices, weights, out_weight, gains)


def from_mp(value, apart):
    return lax.ppermute(value, "mp", [((index + apart) % MP, index) for index in range(MP)])


def from_x(value, apart):
    count = lax.axis_size("pairs")
    pairs = [(index // MP * MP + (index + apart) % MP, index) for index in range(count)]
    return lax.ppermute(value, "pairs", pairs)


def together_kernel(*refs):
    *sources, out_ref, held_ref, in_sems, out_sems = refs
    arriving = []
    for source in sources:
        for kind in range(source.shape[0]):
            place = len(arriving)
            arriving.append(pltpu.make_async_copy(source.at[kind], held_ref.at[place], in_sems.at[place]))
            arriving[place].start()
    leaving = []
    for place, copy in enumerate(arriving):
        copy.wait()
        leaving.append(pltpu.make_async_copy(held_ref.at[place], out_ref.at[place], out_sems.at[place]))
        leaving[place].start()
    for copy in leaving:
        copy.wait()


def together(*weights):
    count = sum(weight.shape[0] for weight in weights)
    shape = (count,) + weights[0].shape[1:]
    return pl.pallas_call(
        together_kernel,
        out_shape=jax.ShapeDtypeStruct(shape, jnp.bfloat16),
        in_specs=in_hbm(len(weights)),
        out_specs=in_hbm(1)[0],
        scratch_shapes=[
            pltpu.VMEM(shape, jnp.bfloat16),
            pltpu.SemaphoreType.DMA((count,)),
            pltpu.SemaphoreType.DMA((count,)),
        ],
        compiler_params=pltpu.CompilerParams(vmem_limit_bytes=MOST_VMEM),
        cost_estimate=estimate(0, 4 * count * COLS * D),
        name="together",
    )(*weights)


def local(
    enc_tokens,
    pair_views,
    embed_weight,
    self_qkv,
    self_out,
    cross_query,
    cross_kv,
    cross_out,
    norm_gains,
    head_weight,
):
    side_index = lax.axis_index("side")
    flip = [(0, 1), (1, 0)]
    weights = together(*(jnp.swapaxes(weight, 1, 2) for weight in (self_qkv[0], cross_kv[0])))
    weights = lax.all_gather(weights, "mp", axis=0)
    mp_index, x_index = lax.axis_index("mp"), lax.axis_index("pairs") % MP
    quarter = lax.dynamic_slice_in_dim(jnp.swapaxes(cross_query[0], 0, 1), x_index * (COLS // MP), COLS // MP)
    quarters = jnp.stack([quarter] + [from_mp(quarter, apart) for apart in APART[1:]])
    spread = lax.all_to_all(
        embed(enc_tokens, embed_weight, side_index), "pairs", split_axis=0, concat_axis=0, tiled=True
    )
    spread, quarters = lax.optimization_barrier((spread, quarters))
    slices = [quarters] + [from_x(quarters, apart) for apart in APART[1:]]
    views = enc_tokens.shape[0]
    taken = views // 2
    own = spread.reshape((-1,) + spread.shape[2:])
    other = lax.ppermute(own, "side", flip)
    wanted = jnp.where(side_index == 0, pair_views[:, 0], pair_views[:, 1])
    within = wanted % views
    slots = wanted // views * taken + within % taken
    slots = jnp.where(within // taken == side_index, slots, slots + own.shape[0])
    packets = pick(slots, own, other)
    pieces = lax.all_to_all(packets, ("pairs", "mp"), split_axis=0, concat_axis=0, tiled=True)
    pieces, slices = lax.optimization_barrier((pieces, slices))
    partner = lax.ppermute(pieces, "side", flip)
    after_self, cross_weights = self_block(pieces, weights, self_out[0], norm_gains[0])
    place = jnp.stack([mp_index, x_index])
    final_rows = cross_block(place, after_self, partner, slices, cross_weights, cross_out[0], norm_gains[0])
    final_rows = lax.all_to_all(
        final_rows.reshape(MP, TOK // MP, D), "mp", split_axis=0, concat_axis=0, tiled=True
    )
    result = jnp.einsum("prd,de->pre", final_rows, head_weight[0], preferred_element_type=jnp.float32)
    return result.astype(jnp.bfloat16)[:, None]


def solution(mesh):
    placed = (
        P("pairs", "mp", None),
        P(),
        P(),
        P("side", None, None, "mp"),
        P("side", None, None),
        P("side", None, "mp"),
        P("side", None, None, "mp"),
        P("side", None, None),
        P("side", None, None),
        P("side", None, None),
    )
    return jax.shard_map(
        local, mesh=mesh, in_specs=placed, out_specs=P("pairs", "side", "mp", None), check_vma=False
    )
```

```python
import jax
import jax.numpy as jnp
from jax import lax
from jax.experimental import pallas as pl
from jax.experimental.pallas import tpu as pltpu
from jax.sharding import PartitionSpec as P

D = 768
HEADS = 12
HEAD_DIM = D // HEADS
TOK = 512
MP = 4
COLS = D // MP
WINDOW = 256
KINDS = 3
PIECE_ROWS = 8
PIECE_COLS = 384
HALVES = D // PIECE_COLS
APART = (0, -1 % MP, 1, 2)
CHUNK = 512
AHEAD = 1
LOG_SCALE = 1.4426950408889634 * HEAD_DIM**-0.5
VMEM = 48 * 2**20
MOST_VMEM = 61 * 2**20


def layer_norm(values, gain):
    average = jnp.mean(values, axis=-1, keepdims=True)
    centred = values - average
    spread = jnp.mean(centred * centred, axis=-1, keepdims=True)
    return centred * lax.rsqrt(spread + 1e-06) * gain


def estimate(flops, moved, exps=0):
    return pl.CostEstimate(flops=int(flops), bytes_accessed=int(moved), transcendentals=int(exps))


def in_vmem(count):
    return [pl.BlockSpec(memory_space=pltpu.VMEM)] * count


def in_hbm(count):
    return [pl.BlockSpec(memory_space=pltpu.HBM)] * count


def embed_kernel(side_ref, tokens_ref, weight_ref, out_ref, held_ref, held_weight_ref, sems):
    views, rows, width = held_ref.shape
    fetched = pltpu.make_async_copy(tokens_ref.at[pl.ds(side_ref[0] * views, views)], held_ref, sems.at[0])
    fetched.start()
    halves = []
    for half in range(HALVES):
        columns = slice(half * PIECE_COLS, (half + 1) * PIECE_COLS)
        halves.append(
            pltpu.make_async_copy(weight_ref.at[:, columns], held_weight_ref.at[:, columns], sems.at[1 + half])
        )
        halves[half].start()
    fetched.wait()
    tokens = held_ref[...].reshape(views * rows, width)
    for half in range(HALVES):
        halves[half].wait()
        columns = slice(half * PIECE_COLS, (half + 1) * PIECE_COLS)
        embedded = jnp.dot(tokens, held_weight_ref[:, columns], preferred_element_type=jnp.float32)
        for view in range(views):
            for block in range(rows // PIECE_ROWS):
                top = view * rows + block * PIECE_ROWS
                out_ref[block * HALVES + half, view] = embedded[top : top + PIECE_ROWS].astype(jnp.bfloat16)


def embed(enc_tokens, embed_weight, side_index):
    views, rows, width = enc_tokens.shape
    taken = views // 2
    pieces = rows // PIECE_ROWS * HALVES
    return pl.pallas_call(
        embed_kernel,
        out_shape=jax.ShapeDtypeStruct((pieces, taken, PIECE_ROWS, PIECE_COLS), jnp.bfloat16),
        in_specs=[pl.BlockSpec(memory_space=pltpu.SMEM)] + [pl.BlockSpec(memory_space=pltpu.HBM)] * 2,
        out_specs=pl.BlockSpec(memory_space=pltpu.VMEM),
        scratch_shapes=[
            pltpu.VMEM((taken, rows, width), jnp.bfloat16),
            pltpu.VMEM((width, D), jnp.bfloat16),
            pltpu.SemaphoreType.DMA((1 + HALVES,)),
        ],
        compiler_params=pltpu.CompilerParams(vmem_limit_bytes=MOST_VMEM),
        cost_estimate=estimate(2 * taken * rows * width * D, 2 * (taken * rows * (width + D) + width * D)),
        name="embed",
    )(side_index.reshape(1), enc_tokens, embed_weight)


def pick_kernel(slots_ref, own_ref, other_ref, out_ref):
    count = own_ref.shape[0]

    def step(pair, carry):
        code = slots_ref[pair]
        foreign = code >= count
        slot = jnp.where(foreign, code - count, code)
        out_ref[pair] = jnp.where(foreign, other_ref[slot], own_ref[slot])
        return carry

    lax.fori_loop(0, out_ref.shape[0], step, 0, unroll=8)


def pick(slots, own, other):
    shape = (slots.shape[0],) + own.shape[1:]
    return pl.pallas_call(
        pick_kernel,
        out_shape=jax.ShapeDtypeStruct(shape, own.dtype),
        in_specs=[
            pl.BlockSpec(memory_space=pltpu.SMEM),
            pl.BlockSpec(memory_space=pltpu.VMEM),
            pl.BlockSpec(memory_space=pltpu.VMEM),
        ],
        out_specs=pl.BlockSpec(memory_space=pltpu.VMEM),
        compiler_params=pltpu.CompilerParams(vmem_limit_bytes=VMEM),
        cost_estimate=estimate(own.size, 6 * own.size),
        name="pick",
    )(slots, own, other)


def unpack(pieces_ref, rows_ref):
    per_device = TOK // MP
    for piece in range(pieces_ref.shape[0]):
        source, owner = divmod(piece, MP)
        block, half = divmod(source, HALVES)
        top = owner * per_device + block * PIECE_ROWS
        rows_ref[top : top + PIECE_ROWS, half * PIECE_COLS : (half + 1) * PIECE_COLS] = pieces_ref[
            piece
        ].astype(jnp.float32)


def normalise(rows_ref, gain, out_ref):
    for top in range(0, TOK, 128):
        out_ref[top : top + 128] = layer_norm(rows_ref[top : top + 128], gain).astype(jnp.bfloat16)


def project(rows, columns_of, quad):
    parts = []
    column = quad * WINDOW
    while column < (quad + 1) * WINDOW:
        owner, first = divmod(column, COLS)
        last = min(COLS, first + (quad + 1) * WINDOW - column)
        parts.append(columns_of(owner, first, last))
        column += last - first
    return lax.dot_general(
        rows, jnp.concatenate(parts, axis=0), (((1,), (1,)), ((), ())), preferred_element_type=jnp.float32
    )


def of_kind(weight_ref, kind):
    return lambda owner, first, last: weight_ref[owner, kind, first:last]


def scores_of(queries, keys, head, top):
    inside = lax.broadcasted_iota(jnp.int32, (1, WINDOW), 1) // HEAD_DIM == head
    masked = jnp.where(inside, queries[top : top + CHUNK], 0.0).astype(jnp.bfloat16)
    return lax.dot_general(masked, keys, (((1,), (1,)), ((), ())), preferred_element_type=jnp.float32)


def attend(quad_of, attended_ref):
    steps = [
        (quad, head, top)
        for quad in range(D // WINDOW)
        for head in range(WINDOW // HEAD_DIM)
        for top in range(0, TOK, CHUNK)
    ]
    lane = lax.broadcasted_iota(jnp.int32, (1, WINDOW), 1)
    held = {}
    sums = {}

    def start(step):
        quad, head, top = step
        if quad not in held:
            queries, keys, values = quad_of(quad)
            held[quad] = (queries * LOG_SCALE, keys.astype(jnp.bfloat16), values.astype(jnp.bfloat16))
        return scores_of(held[quad][0], held[quad][1], head, top)

    ahead = [start(step) for step in steps[:AHEAD]]
    for count, (quad, head, top) in enumerate(steps):
        if count + AHEAD < len(steps):
            ahead.append(start(steps[count + AHEAD]))
        scores = ahead.pop(0)
        weights = jnp.exp2(scores - jnp.max(scores, axis=-1, keepdims=True))
        total = jnp.sum(weights, axis=-1, keepdims=True)
        mixture = jnp.dot(weights.astype(jnp.bfloat16), held[quad][2], preferred_element_type=jnp.float32)
        mixture = mixture * (1.0 / total)
        if head:
            mixture = jnp.where(lane // HEAD_DIM == head, mixture, sums[quad, top])
        sums[quad, top] = mixture
        if head == WINDOW // HEAD_DIM - 1:
            attended_ref[top : top + CHUNK, quad * WINDOW : (quad + 1) * WINDOW] = mixture.astype(jnp.bfloat16)


def fetch(gathered_ref, first_kind, weight_ref, sems):
    kinds = weight_ref.shape[1]
    waiting = []
    for owner in range(MP):
        source = gathered_ref.at[owner, first_kind : first_kind + kinds]
        waiting.append(pltpu.make_async_copy(source, weight_ref.at[owner], sems.at[owner]))
        waiting[owner].start()

    def ready(quad):
        last = ((quad + 1) * WINDOW - 1) // COLS
        while waiting and MP - len(waiting) <= last:
            waiting.pop(0).wait()

    return ready


def self_kernel(
    pieces_ref, gathered_ref, out_weight_ref, gain_ref, out_ref, normed_ref, attended_ref, weight_ref, sems
):
    ready = fetch(gathered_ref, 0, weight_ref, sems)
    unpack(pieces_ref, out_ref)
    normalise(out_ref, gain_ref[0:1], normed_ref)
    normed = normed_ref[...]

    def quad_of(quad):
        ready(quad)
        return [project(normed, of_kind(weight_ref, kind), quad) for kind in range(KINDS)]

    attend(quad_of, attended_ref)
    out_ref[...] += jnp.dot(attended_ref[...], out_weight_ref[...], preferred_element_type=jnp.float32)


def cross_kernel(
    place_ref, after_ref, pieces_ref, slices0_ref, slices1_ref, slices2_ref, slices3_ref, gathered_ref, out_weight_ref,
    gain_ref, out_ref, rows_ref, query_ref, partner_ref, attended_ref, slices_ref, weight_ref, slice_sems, sems,
):
    fetched = []
    for count, source in enumerate((slices0_ref, slices1_ref, slices2_ref, slices3_ref)):
        along_x = lax.rem(place_ref[1] + APART[count], MP)
        for place in range(MP):
            owner = lax.rem(place_ref[0] + APART[place], MP)
            sem = slice_sems.at[count * MP + place]
            fetched.append(pltpu.make_async_copy(source.at[place], slices_ref.at[owner, along_x], sem))
            fetched[-1].start()
    ready = fetch(gathered_ref, KINDS, weight_ref, sems)
    unpack(pieces_ref, rows_ref)
    normalise(rows_ref, gain_ref[2:3], partner_ref)
    normalise(after_ref, gain_ref[1:2], query_ref)
    queries, partner = query_ref[...], partner_ref[...]
    for copy in fetched:
        copy.wait()

    def query_columns(owner, first, last):
        return slices_ref[owner].reshape(COLS, D)[first:last]

    def quad_of(quad):
        ready(quad)
        return (
            project(queries, query_columns, quad),
            project(partner, of_kind(weight_ref, 0), quad),
            project(partner, of_kind(weight_ref, 1), quad),
        )

    attend(quad_of, attended_ref)
    rows_ref[...] = after_ref[...] + jnp.dot(
        attended_ref[...], out_weight_ref[...], preferred_element_type=jnp.float32
    )
    normalise(rows_ref, gain_ref[3:4], out_ref)


def self_block(pieces, weights, out_weight, gains):
    return pl.pallas_call(
        self_kernel,
        out_shape=jax.ShapeDtypeStruct((TOK, D), jnp.float32),
        in_specs=in_vmem(1) + in_hbm(1) + in_vmem(2),
        out_specs=in_vmem(1)[0],
        scratch_shapes=[pltpu.VMEM((TOK, D), jnp.bfloat16)] * 2
        + [pltpu.VMEM((MP, KINDS, COLS, D), jnp.bfloat16), pltpu.SemaphoreType.DMA((MP,))],
        compiler_params=pltpu.CompilerParams(vmem_limit_bytes=VMEM),
        cost_estimate=estimate(8 * TOK * D * D + 4 * TOK * TOK * D, 8 * 2**20, HEADS * TOK * TOK),
        name="self_block",
    )(pieces, weights, out_weight, gains)


def cross_block(place, after_self, pieces, slices, weights, out_weight, gains):
    kinds = weights.shape[1] - KINDS
    return pl.pallas_call(
        cross_kernel,
        out_shape=jax.ShapeDtypeStruct((TOK, D), jnp.bfloat16),
        in_specs=[pl.BlockSpec(memory_space=pltpu.SMEM)] + in_vmem(2) + in_hbm(MP + 1) + in_vmem(2),
        out_specs=in_vmem(1)[0],
        scratch_shapes=[pltpu.VMEM((TOK, D), jnp.float32)]
        + [pltpu.VMEM((TOK, D), jnp.bfloat16)] * 3
        + [
            pltpu.VMEM((MP,) + slices[0].shape, jnp.bfloat16),
            pltpu.VMEM((MP, kinds, COLS, D), jnp.bfloat16),
            pltpu.SemaphoreType.DMA((MP * MP,)),
            pltpu.SemaphoreType.DMA((MP,)),
        ],
        compiler_params=pltpu.CompilerParams(vmem_limit_bytes=VMEM),
        cost_estimate=estimate(8 * TOK * D * D + 4 * TOK * TOK * D, 8 * 2**20, HEADS * TOK * TOK),
        name="cross_block",
    )(place, after_self, pieces, *slices, weights, out_weight, gains)


def from_mp(value, apart):
    return lax.ppermute(value, "mp", [((index + apart) % MP, index) for index in range(MP)])


def from_x(value, apart):
    count = lax.axis_size("pairs")
    pairs = [(index // MP * MP + (index + apart) % MP, index) for index in range(count)]
    return lax.ppermute(value, "pairs", pairs)


def together_kernel(*refs):
    *sources, out_ref, held_ref, in_sems, out_sems = refs
    arriving = []
    for source in sources:
        for kind in range(source.shape[0]):
            place = len(arriving)
            arriving.append(pltpu.make_async_copy(source.at[kind], held_ref.at[place], in_sems.at[place]))
            arriving[place].start()
    leaving = []
    for place, copy in enumerate(arriving):
        copy.wait()
        leaving.append(pltpu.make_async_copy(held_ref.at[place], out_ref.at[place], out_sems.at[place]))
        leaving[place].start()
    for copy in leaving:
        copy.wait()


def together(*weights):
    count = sum(weight.shape[0] for weight in weights)
    shape = (count,) + weights[0].shape[1:]
    return pl.pallas_call(
        together_kernel,
        out_shape=jax.ShapeDtypeStruct(shape, jnp.bfloat16),
        in_specs=in_hbm(len(weights)),
        out_specs=in_hbm(1)[0],
        scratch_shapes=[
            pltpu.VMEM(shape, jnp.bfloat16),
            pltpu.SemaphoreType.DMA((count,)),
            pltpu.SemaphoreType.DMA((count,)),
        ],
        compiler_params=pltpu.CompilerParams(vmem_limit_bytes=MOST_VMEM),
        cost_estimate=estimate(0, 4 * count * COLS * D),
        name="together",
    )(*weights)


def local(
    enc_tokens,
    pair_views,
    embed_weight,
    self_qkv,
    self_out,
    cross_query,
    cross_kv,
    cross_out,
    norm_gains,
    head_weight,
):
    side_index = lax.axis_index("side")
    flip = [(0, 1), (1, 0)]
    weights = together(*(jnp.swapaxes(weight, 1, 2) for weight in (self_qkv[0], cross_kv[0])))
    weights = lax.all_gather(weights, "mp", axis=0)
    mp_index, x_index = lax.axis_index("mp"), lax.axis_index("pairs") % MP
    quarter = lax.dynamic_slice_in_dim(jnp.swapaxes(cross_query[0], 0, 1), x_index * (COLS // MP), COLS // MP)
    quarters = jnp.stack([quarter] + [from_mp(quarter, apart) for apart in APART[1:]])
    spread = lax.all_to_all(
        embed(enc_tokens, embed_weight, side_index), "pairs", split_axis=0, concat_axis=0, tiled=True
    )
    spread, quarters = lax.optimization_barrier((spread, quarters))
    slices = [quarters] + [from_x(quarters, apart) for apart in APART[1:]]
    views = enc_tokens.shape[0]
    taken = views // 2
    own = spread.reshape((-1,) + spread.shape[2:])
    other = lax.ppermute(own, "side", flip)
    wanted = jnp.where(side_index == 0, pair_views[:, 0], pair_views[:, 1])
    within = wanted % views
    slots = wanted // views * taken + within % taken
    slots = jnp.where(within // taken == side_index, slots, slots + own.shape[0])
    packets = pick(slots, own, other)
    pieces = lax.all_to_all(packets, ("pairs", "mp"), split_axis=0, concat_axis=0, tiled=True)
    pieces, slices = lax.optimization_barrier((pieces, slices))
    partner = lax.ppermute(pieces, "side", flip)
    after_self = self_block(pieces, weights, self_out[0], norm_gains[0])
    place = jnp.stack([mp_index, x_index])
    final_rows = cross_block(place, after_self, partner, slices, weights, cross_out[0], norm_gains[0])
    final_rows = lax.all_to_all(
        final_rows.reshape(MP, TOK // MP, D), "mp", split_axis=0, concat_axis=0, tiled=True
    )
    result = jnp.einsum("prd,de->pre", final_rows, head_weight[0], preferred_element_type=jnp.float32)
    return result.astype(jnp.bfloat16)[:, None]


def solution(mesh):
    placed = (
        P("pairs", "mp", None),
        P(),
        P(),
        P("side", None, None, "mp"),
        P("side", None, None),
        P("side", None, "mp"),
        P("side", None, None, "mp"),
        P("side", None, None),
        P("side", None, None),
        P("side", None, None),
    )
    return jax.shard_map(
        local, mesh=mesh, in_specs=placed, out_specs=P("pairs", "side", "mp", None), check_vma=False
    )
```

```python
import jax
import jax.numpy as jnp
from jax import lax
from jax.experimental import pallas as pl
from jax.experimental.pallas import tpu as pltpu
from jax.sharding import PartitionSpec as P

D = 768
HEADS = 12
HEAD_DIM = D // HEADS
TOK = 512
MP = 4
COLS = D // MP
WINDOW = 256
KINDS = 3
PIECE_ROWS = 8
PIECE_COLS = 384
HALVES = D // PIECE_COLS
CHUNK = 512
AHEAD = 1
LOG_SCALE = 1.4426950408889634 * HEAD_DIM**-0.5
VMEM = 48 * 2**20
MOST_VMEM = 61 * 2**20


def layer_norm(values, gain):
    average = jnp.mean(values, axis=-1, keepdims=True)
    centred = values - average
    spread = jnp.mean(centred * centred, axis=-1, keepdims=True)
    return centred * lax.rsqrt(spread + 1e-06) * gain


def estimate(flops, moved, exps=0):
    return pl.CostEstimate(flops=int(flops), bytes_accessed=int(moved), transcendentals=int(exps))


def in_vmem(count):
    return [pl.BlockSpec(memory_space=pltpu.VMEM)] * count


def in_hbm(count):
    return [pl.BlockSpec(memory_space=pltpu.HBM)] * count


def embed_kernel(side_ref, tokens_ref, weight_ref, out_ref, held_ref, held_weight_ref, sems):
    views, rows, width = held_ref.shape
    fetched = pltpu.make_async_copy(tokens_ref.at[pl.ds(side_ref[0] * views, views)], held_ref, sems.at[0])
    fetched.start()
    halves = []
    for half in range(HALVES):
        columns = slice(half * PIECE_COLS, (half + 1) * PIECE_COLS)
        halves.append(
            pltpu.make_async_copy(weight_ref.at[:, columns], held_weight_ref.at[:, columns], sems.at[1 + half])
        )
        halves[half].start()
    fetched.wait()
    tokens = held_ref[...].reshape(views * rows, width)
    for half in range(HALVES):
        halves[half].wait()
        columns = slice(half * PIECE_COLS, (half + 1) * PIECE_COLS)
        embedded = jnp.dot(tokens, held_weight_ref[:, columns], preferred_element_type=jnp.float32)
        for view in range(views):
            for block in range(rows // PIECE_ROWS):
                top = view * rows + block * PIECE_ROWS
                out_ref[block * HALVES + half, view] = embedded[top : top + PIECE_ROWS].astype(jnp.bfloat16)


def embed(enc_tokens, embed_weight, side_index):
    views, rows, width = enc_tokens.shape
    taken = views // 2
    pieces = rows // PIECE_ROWS * HALVES
    return pl.pallas_call(
        embed_kernel,
        out_shape=jax.ShapeDtypeStruct((pieces, taken, PIECE_ROWS, PIECE_COLS), jnp.bfloat16),
        in_specs=[pl.BlockSpec(memory_space=pltpu.SMEM)] + [pl.BlockSpec(memory_space=pltpu.HBM)] * 2,
        out_specs=pl.BlockSpec(memory_space=pltpu.VMEM),
        scratch_shapes=[
            pltpu.VMEM((taken, rows, width), jnp.bfloat16),
            pltpu.VMEM((width, D), jnp.bfloat16),
            pltpu.SemaphoreType.DMA((1 + HALVES,)),
        ],
        compiler_params=pltpu.CompilerParams(vmem_limit_bytes=MOST_VMEM),
        cost_estimate=estimate(2 * taken * rows * width * D, 2 * (taken * rows * (width + D) + width * D)),
        name="embed",
    )(side_index.reshape(1), enc_tokens, embed_weight)


def pick_kernel(slots_ref, own_ref, other_ref, out_ref):
    count = own_ref.shape[0]

    def step(pair, carry):
        code = slots_ref[pair]
        foreign = code >= count
        slot = jnp.where(foreign, code - count, code)
        out_ref[pair] = jnp.where(foreign, other_ref[slot], own_ref[slot])
        return carry

    lax.fori_loop(0, out_ref.shape[0], step, 0, unroll=8)


def pick(slots, own, other):
    shape = (slots.shape[0],) + own.shape[1:]
    return pl.pallas_call(
        pick_kernel,
        out_shape=jax.ShapeDtypeStruct(shape, own.dtype),
        in_specs=[
            pl.BlockSpec(memory_space=pltpu.SMEM),
            pl.BlockSpec(memory_space=pltpu.VMEM),
            pl.BlockSpec(memory_space=pltpu.VMEM),
        ],
        out_specs=pl.BlockSpec(memory_space=pltpu.VMEM),
        compiler_params=pltpu.CompilerParams(vmem_limit_bytes=VMEM),
        cost_estimate=estimate(own.size, 6 * own.size),
        name="pick",
    )(slots, own, other)


def unpack(pieces_ref, rows_ref):
    per_device = TOK // MP
    for piece in range(pieces_ref.shape[0]):
        source, owner = divmod(piece, MP)
        block, half = divmod(source, HALVES)
        top = owner * per_device + block * PIECE_ROWS
        rows_ref[top : top + PIECE_ROWS, half * PIECE_COLS : (half + 1) * PIECE_COLS] = pieces_ref[
            piece
        ].astype(jnp.float32)


def normalise(rows_ref, gain, out_ref):
    for top in range(0, TOK, 128):
        out_ref[top : top + 128] = layer_norm(rows_ref[top : top + 128], gain).astype(jnp.bfloat16)


def project(rows, columns_of, quad):
    parts = []
    column = quad * WINDOW
    while column < (quad + 1) * WINDOW:
        owner, first = divmod(column, COLS)
        last = min(COLS, first + (quad + 1) * WINDOW - column)
        parts.append(columns_of(owner, first, last))
        column += last - first
    return lax.dot_general(
        rows, jnp.concatenate(parts, axis=0), (((1,), (1,)), ((), ())), preferred_element_type=jnp.float32
    )


def of_kind(weight_ref, kind):
    return lambda owner, first, last: weight_ref[owner, kind, first:last]


def scores_of(queries, keys, head, top):
    inside = lax.broadcasted_iota(jnp.int32, (1, WINDOW), 1) // HEAD_DIM == head
    masked = jnp.where(inside, queries[top : top + CHUNK], 0.0).astype(jnp.bfloat16)
    return lax.dot_general(masked, keys, (((1,), (1,)), ((), ())), preferred_element_type=jnp.float32)


def attend(quad_of, attended_ref):
    steps = [
        (quad, head, top)
        for quad in range(D // WINDOW)
        for head in range(WINDOW // HEAD_DIM)
        for top in range(0, TOK, CHUNK)
    ]
    lane = lax.broadcasted_iota(jnp.int32, (1, WINDOW), 1)
    held = {}
    sums = {}

    def start(step):
        quad, head, top = step
        if quad not in held:
            queries, keys, values = quad_of(quad)
            held[quad] = (queries * LOG_SCALE, keys.astype(jnp.bfloat16), values.astype(jnp.bfloat16))
        return scores_of(held[quad][0], held[quad][1], head, top)

    ahead = [start(step) for step in steps[:AHEAD]]
    for count, (quad, head, top) in enumerate(steps):
        if count + AHEAD < len(steps):
            ahead.append(start(steps[count + AHEAD]))
        scores = ahead.pop(0)
        weights = jnp.exp2(scores - jnp.max(scores, axis=-1, keepdims=True))
        total = jnp.sum(weights, axis=-1, keepdims=True)
        mixture = jnp.dot(weights.astype(jnp.bfloat16), held[quad][2], preferred_element_type=jnp.float32)
        mixture = mixture * (1.0 / total)
        if head:
            mixture = jnp.where(lane // HEAD_DIM == head, mixture, sums[quad, top])
        sums[quad, top] = mixture
        if head == WINDOW // HEAD_DIM - 1:
            attended_ref[top : top + CHUNK, quad * WINDOW : (quad + 1) * WINDOW] = mixture.astype(jnp.bfloat16)


def fetch(gathered_ref, first_kind, weight_ref, sems):
    kinds = weight_ref.shape[1]
    waiting = []
    for owner in range(MP):
        source = gathered_ref.at[owner, first_kind : first_kind + kinds]
        waiting.append(pltpu.make_async_copy(source, weight_ref.at[owner], sems.at[owner]))
        waiting[owner].start()

    def ready(quad):
        last = ((quad + 1) * WINDOW - 1) // COLS
        while waiting and MP - len(waiting) <= last:
            waiting.pop(0).wait()

    return ready


def self_kernel(
    pieces_ref, gathered_ref, out_weight_ref, gain_ref, out_ref, normed_ref, attended_ref, weight_ref, sems
):
    ready = fetch(gathered_ref, 0, weight_ref, sems)
    unpack(pieces_ref, out_ref)
    normalise(out_ref, gain_ref[0:1], normed_ref)
    normed = normed_ref[...]

    def quad_of(quad):
        ready(quad)
        return [project(normed, of_kind(weight_ref, kind), quad) for kind in range(KINDS)]

    attend(quad_of, attended_ref)
    out_ref[...] += jnp.dot(attended_ref[...], out_weight_ref[...], preferred_element_type=jnp.float32)


def cross_kernel(
    place_ref, after_ref, pieces_ref, slices0_ref, slices1_ref, slices2_ref, slices3_ref, gathered_ref, out_weight_ref,
    gain_ref, out_ref, rows_ref, query_ref, partner_ref, attended_ref, slices_ref, weight_ref, slice_sems, sems,
):
    fetched = []
    for count, source in enumerate((slices0_ref, slices1_ref, slices2_ref, slices3_ref)):
        along_x = lax.rem(place_ref[0] + count, MP)
        fetched.append(pltpu.make_async_copy(source, slices_ref.at[:, along_x], slice_sems.at[count]))
        fetched[count].start()
    ready = fetch(gathered_ref, KINDS, weight_ref, sems)
    unpack(pieces_ref, rows_ref)
    normalise(rows_ref, gain_ref[2:3], partner_ref)
    normalise(after_ref, gain_ref[1:2], query_ref)
    queries, partner = query_ref[...], partner_ref[...]
    for copy in fetched:
        copy.wait()

    def query_columns(owner, first, last):
        return slices_ref[owner].reshape(COLS, D)[first:last]

    def quad_of(quad):
        ready(quad)
        return (
            project(queries, query_columns, quad),
            project(partner, of_kind(weight_ref, 0), quad),
            project(partner, of_kind(weight_ref, 1), quad),
        )

    attend(quad_of, attended_ref)
    rows_ref[...] = after_ref[...] + jnp.dot(
        attended_ref[...], out_weight_ref[...], preferred_element_type=jnp.float32
    )
    normalise(rows_ref, gain_ref[3:4], out_ref)


def self_block(pieces, weights, out_weight, gains):
    return pl.pallas_call(
        self_kernel,
        out_shape=jax.ShapeDtypeStruct((TOK, D), jnp.float32),
        in_specs=in_vmem(1) + in_hbm(1) + in_vmem(2),
        out_specs=in_vmem(1)[0],
        scratch_shapes=[pltpu.VMEM((TOK, D), jnp.bfloat16)] * 2
        + [pltpu.VMEM((MP, KINDS, COLS, D), jnp.bfloat16), pltpu.SemaphoreType.DMA((MP,))],
        compiler_params=pltpu.CompilerParams(vmem_limit_bytes=VMEM),
        cost_estimate=estimate(8 * TOK * D * D + 4 * TOK * TOK * D, 8 * 2**20, HEADS * TOK * TOK),
        name="self_block",
    )(pieces, weights, out_weight, gains)


def cross_block(place, after_self, pieces, slices, weights, out_weight, gains):
    kinds = weights.shape[1] - KINDS
    return pl.pallas_call(
        cross_kernel,
        out_shape=jax.ShapeDtypeStruct((TOK, D), jnp.bfloat16),
        in_specs=[pl.BlockSpec(memory_space=pltpu.SMEM)] + in_vmem(2) + in_hbm(MP + 1) + in_vmem(2),
        out_specs=in_vmem(1)[0],
        scratch_shapes=[pltpu.VMEM((TOK, D), jnp.float32)]
        + [pltpu.VMEM((TOK, D), jnp.bfloat16)] * 3
        + [
            pltpu.VMEM((MP,) + slices[0].shape, jnp.bfloat16),
            pltpu.VMEM((MP, kinds, COLS, D), jnp.bfloat16),
            pltpu.SemaphoreType.DMA((MP,)),
            pltpu.SemaphoreType.DMA((MP,)),
        ],
        compiler_params=pltpu.CompilerParams(vmem_limit_bytes=VMEM),
        cost_estimate=estimate(8 * TOK * D * D + 4 * TOK * TOK * D, 8 * 2**20, HEADS * TOK * TOK),
        name="cross_block",
    )(place, after_self, pieces, *slices, weights, out_weight, gains)


def from_mp(value, apart):
    return lax.ppermute(value, "mp", [((index + apart) % MP, index) for index in range(MP)])


def from_x(value, apart):
    count = lax.axis_size("pairs")
    pairs = [(index // MP * MP + (index + apart) % MP, index) for index in range(count)]
    return lax.ppermute(value, "pairs", pairs)


def together_kernel(*refs):
    *sources, out_ref, held_ref, in_sems, out_sems = refs
    arriving = []
    for source in sources:
        for kind in range(source.shape[0]):
            place = len(arriving)
            arriving.append(pltpu.make_async_copy(source.at[kind], held_ref.at[place], in_sems.at[place]))
            arriving[place].start()
    leaving = []
    for place, copy in enumerate(arriving):
        copy.wait()
        leaving.append(pltpu.make_async_copy(held_ref.at[place], out_ref.at[place], out_sems.at[place]))
        leaving[place].start()
    for copy in leaving:
        copy.wait()


def together(*weights):
    count = sum(weight.shape[0] for weight in weights)
    shape = (count,) + weights[0].shape[1:]
    return pl.pallas_call(
        together_kernel,
        out_shape=jax.ShapeDtypeStruct(shape, jnp.bfloat16),
        in_specs=in_hbm(len(weights)),
        out_specs=in_hbm(1)[0],
        scratch_shapes=[
            pltpu.VMEM(shape, jnp.bfloat16),
            pltpu.SemaphoreType.DMA((count,)),
            pltpu.SemaphoreType.DMA((count,)),
        ],
        compiler_params=pltpu.CompilerParams(vmem_limit_bytes=MOST_VMEM),
        cost_estimate=estimate(0, 4 * count * COLS * D),
        name="together",
    )(*weights)


def local(
    enc_tokens,
    pair_views,
    embed_weight,
    self_qkv,
    self_out,
    cross_query,
    cross_kv,
    cross_out,
    norm_gains,
    head_weight,
):
    side_index = lax.axis_index("side")
    flip = [(0, 1), (1, 0)]
    weights = together(*(jnp.swapaxes(weight, 1, 2) for weight in (self_qkv[0], cross_kv[0])))
    weights = lax.all_gather(weights, "mp", axis=0)
    mp_index, x_index = lax.axis_index("mp"), lax.axis_index("pairs") % MP
    quarter = lax.dynamic_slice_in_dim(jnp.swapaxes(cross_query[0], 0, 1), x_index * (COLS // MP), COLS // MP)
    quarters = [quarter] + [from_mp(quarter, apart) for apart in range(1, MP)]
    quarters = jnp.stack([lax.select_n((owner - mp_index) % MP, *quarters) for owner in range(MP)])
    spread = lax.all_to_all(
        embed(enc_tokens, embed_weight, side_index), "pairs", split_axis=0, concat_axis=0, tiled=True
    )
    spread, quarters = lax.optimization_barrier((spread, quarters))
    slices = [quarters] + [from_x(quarters, apart) for apart in range(1, MP)]
    views = enc_tokens.shape[0]
    taken = views // 2
    own = spread.reshape((-1,) + spread.shape[2:])
    other = lax.ppermute(own, "side", flip)
    wanted = jnp.where(side_index == 0, pair_views[:, 0], pair_views[:, 1])
    within = wanted % views
    slots = wanted // views * taken + within % taken
    slots = jnp.where(within // taken == side_index, slots, slots + own.shape[0])
    packets = pick(slots, own, other)
    pieces = lax.all_to_all(packets, ("pairs", "mp"), split_axis=0, concat_axis=0, tiled=True)
    pieces, slices = lax.optimization_barrier((pieces, slices))
    partner = lax.ppermute(pieces, "side", flip)
    after_self = self_block(pieces, weights, self_out[0], norm_gains[0])
    place = x_index.reshape(1)
    final_rows = cross_block(place, after_self, partner, slices, weights, cross_out[0], norm_gains[0])
    final_rows = lax.all_to_all(
        final_rows.reshape(MP, TOK // MP, D), "mp", split_axis=0, concat_axis=0, tiled=True
    )
    result = jnp.einsum("prd,de->pre", final_rows, head_weight[0], preferred_element_type=jnp.float32)
    return result.astype(jnp.bfloat16)[:, None]


def solution(mesh):
    placed = (
        P("pairs", "mp", None),
        P(),
        P(),
        P("side", None, None, "mp"),
        P("side", None, None),
        P("side", None, "mp"),
        P("side", None, None, "mp"),
        P("side", None, None),
        P("side", None, None),
        P("side", None, None),
    )
    return jax.shard_map(
        local, mesh=mesh, in_specs=placed, out_specs=P("pairs", "side", "mp", None), check_vma=False
    )
```

```python
import jax
import jax.numpy as jnp
from jax import lax
from jax.experimental import pallas as pl
from jax.experimental.pallas import tpu as pltpu
from jax.sharding import PartitionSpec as P

D = 768
HEADS = 12
HEAD_DIM = D // HEADS
TOK = 512
MP = 4
COLS = D // MP
WINDOW = 256
KINDS = 3
PIECE_ROWS = 8
PIECE_COLS = 384
HALVES = D // PIECE_COLS
CHUNK = 512
AHEAD = 1
LOG_SCALE = 1.4426950408889634 * HEAD_DIM**-0.5
VMEM = 48 * 2**20
MOST_VMEM = 61 * 2**20


def layer_norm(values, gain):
    average = jnp.mean(values, axis=-1, keepdims=True)
    centred = values - average
    spread = jnp.mean(centred * centred, axis=-1, keepdims=True)
    return centred * lax.rsqrt(spread + 1e-06) * gain


def estimate(flops, moved, exps=0):
    return pl.CostEstimate(flops=int(flops), bytes_accessed=int(moved), transcendentals=int(exps))


def in_vmem(count):
    return [pl.BlockSpec(memory_space=pltpu.VMEM)] * count


def in_hbm(count):
    return [pl.BlockSpec(memory_space=pltpu.HBM)] * count


def embed_kernel(side_ref, tokens_ref, weight_ref, out_ref, held_ref, held_weight_ref, sems):
    views, rows, width = held_ref.shape
    fetched = pltpu.make_async_copy(tokens_ref.at[pl.ds(side_ref[0] * views, views)], held_ref, sems.at[0])
    fetched.start()
    halves = []
    for half in range(HALVES):
        columns = slice(half * PIECE_COLS, (half + 1) * PIECE_COLS)
        halves.append(
            pltpu.make_async_copy(weight_ref.at[:, columns], held_weight_ref.at[:, columns], sems.at[1 + half])
        )
        halves[half].start()
    fetched.wait()
    tokens = held_ref[...].reshape(views * rows, width)
    for half in range(HALVES):
        halves[half].wait()
        columns = slice(half * PIECE_COLS, (half + 1) * PIECE_COLS)
        embedded = jnp.dot(tokens, held_weight_ref[:, columns], preferred_element_type=jnp.float32)
        for view in range(views):
            for block in range(rows // PIECE_ROWS):
                top = view * rows + block * PIECE_ROWS
                out_ref[block * HALVES + half, view] = embedded[top : top + PIECE_ROWS].astype(jnp.bfloat16)


def embed(enc_tokens, embed_weight, side_index):
    views, rows, width = enc_tokens.shape
    taken = views // 2
    pieces = rows // PIECE_ROWS * HALVES
    return pl.pallas_call(
        embed_kernel,
        out_shape=jax.ShapeDtypeStruct((pieces, taken, PIECE_ROWS, PIECE_COLS), jnp.bfloat16),
        in_specs=[pl.BlockSpec(memory_space=pltpu.SMEM)] + [pl.BlockSpec(memory_space=pltpu.HBM)] * 2,
        out_specs=pl.BlockSpec(memory_space=pltpu.VMEM),
        scratch_shapes=[
            pltpu.VMEM((taken, rows, width), jnp.bfloat16),
            pltpu.VMEM((width, D), jnp.bfloat16),
            pltpu.SemaphoreType.DMA((1 + HALVES,)),
        ],
        compiler_params=pltpu.CompilerParams(vmem_limit_bytes=MOST_VMEM),
        cost_estimate=estimate(2 * taken * rows * width * D, 2 * (taken * rows * (width + D) + width * D)),
        name="embed",
    )(side_index.reshape(1), enc_tokens, embed_weight)


def pick_kernel(slots_ref, own_ref, other_ref, out_ref):
    count = own_ref.shape[0]

    def step(pair, carry):
        code = slots_ref[pair]
        foreign = code >= count
        slot = jnp.where(foreign, code - count, code)
        out_ref[pair] = jnp.where(foreign, other_ref[slot], own_ref[slot])
        return carry

    lax.fori_loop(0, out_ref.shape[0], step, 0, unroll=32)


def pick(slots, own, other):
    shape = (slots.shape[0],) + own.shape[1:]
    return pl.pallas_call(
        pick_kernel,
        out_shape=jax.ShapeDtypeStruct(shape, own.dtype),
        in_specs=[
            pl.BlockSpec(memory_space=pltpu.SMEM),
            pl.BlockSpec(memory_space=pltpu.VMEM),
            pl.BlockSpec(memory_space=pltpu.VMEM),
        ],
        out_specs=pl.BlockSpec(memory_space=pltpu.VMEM),
        compiler_params=pltpu.CompilerParams(vmem_limit_bytes=VMEM),
        cost_estimate=estimate(own.size, 6 * own.size),
        name="pick",
    )(slots, own, other)


def unpack(pieces_ref, rows_ref):
    per_device = TOK // MP
    for piece in range(pieces_ref.shape[0]):
        source, owner = divmod(piece, MP)
        block, half = divmod(source, HALVES)
        top = owner * per_device + block * PIECE_ROWS
        rows_ref[top : top + PIECE_ROWS, half * PIECE_COLS : (half + 1) * PIECE_COLS] = pieces_ref[
            piece
        ].astype(jnp.float32)


def normalise(rows_ref, gain, out_ref):
    for top in range(0, TOK, 128):
        out_ref[top : top + 128] = layer_norm(rows_ref[top : top + 128], gain).astype(jnp.bfloat16)


def project(rows, columns_of, quad):
    parts = []
    column = quad * WINDOW
    while column < (quad + 1) * WINDOW:
        owner, first = divmod(column, COLS)
        last = min(COLS, first + (quad + 1) * WINDOW - column)
        parts.append(columns_of(owner, first, last))
        column += last - first
    return lax.dot_general(
        rows, jnp.concatenate(parts, axis=0), (((1,), (1,)), ((), ())), preferred_element_type=jnp.float32
    )


def of_kind(weight_ref, kind):
    return lambda owner, first, last: weight_ref[owner, kind, first:last]


def scores_of(queries, keys, head, top):
    inside = lax.broadcasted_iota(jnp.int32, (1, WINDOW), 1) // HEAD_DIM == head
    masked = jnp.where(inside, queries[top : top + CHUNK], 0.0).astype(jnp.bfloat16)
    return lax.dot_general(masked, keys, (((1,), (1,)), ((), ())), preferred_element_type=jnp.float32)


def attend(quad_of, attended_ref):
    steps = [
        (quad, head, top)
        for quad in range(D // WINDOW)
        for head in range(WINDOW // HEAD_DIM)
        for top in range(0, TOK, CHUNK)
    ]
    lane = lax.broadcasted_iota(jnp.int32, (1, WINDOW), 1)
    held = {}
    sums = {}

    def start(step):
        quad, head, top = step
        if quad not in held:
            queries, keys, values = quad_of(quad)
            held[quad] = (queries * LOG_SCALE, keys.astype(jnp.bfloat16), values.astype(jnp.bfloat16))
        return scores_of(held[quad][0], held[quad][1], head, top)

    ahead = [start(step) for step in steps[:AHEAD]]
    for count, (quad, head, top) in enumerate(steps):
        if count + AHEAD < len(steps):
            ahead.append(start(steps[count + AHEAD]))
        scores = ahead.pop(0)
        weights = jnp.exp2(scores - jnp.max(scores, axis=-1, keepdims=True))
        total = jnp.sum(weights, axis=-1, keepdims=True)
        mixture = jnp.dot(weights.astype(jnp.bfloat16), held[quad][2], preferred_element_type=jnp.float32)
        mixture = mixture * (1.0 / total)
        if head:
            mixture = jnp.where(lane // HEAD_DIM == head, mixture, sums[quad, top])
        sums[quad, top] = mixture
        if head == WINDOW // HEAD_DIM - 1:
            attended_ref[top : top + CHUNK, quad * WINDOW : (quad + 1) * WINDOW] = mixture.astype(jnp.bfloat16)


def fetch(gathered_ref, first_kind, weight_ref, sems):
    kinds = weight_ref.shape[1]
    waiting = []
    for owner in range(MP):
        source = gathered_ref.at[owner, first_kind : first_kind + kinds]
        waiting.append(pltpu.make_async_copy(source, weight_ref.at[owner], sems.at[owner]))
        waiting[owner].start()

    def ready(quad):
        last = ((quad + 1) * WINDOW - 1) // COLS
        while waiting and MP - len(waiting) <= last:
            waiting.pop(0).wait()

    return ready


def self_kernel(
    pieces_ref, gathered_ref, out_weight_ref, gain_ref, out_ref, normed_ref, attended_ref, weight_ref, sems
):
    ready = fetch(gathered_ref, 0, weight_ref, sems)
    unpack(pieces_ref, out_ref)
    normalise(out_ref, gain_ref[0:1], normed_ref)
    normed = normed_ref[...]

    def quad_of(quad):
        ready(quad)
        return [project(normed, of_kind(weight_ref, kind), quad) for kind in range(KINDS)]

    attend(quad_of, attended_ref)
    out_ref[...] += jnp.dot(attended_ref[...], out_weight_ref[...], preferred_element_type=jnp.float32)


def cross_kernel(
    place_ref, after_ref, pieces_ref, slices0_ref, slices1_ref, slices2_ref, slices3_ref, gathered_ref, out_weight_ref,
    gain_ref, out_ref, rows_ref, query_ref, partner_ref, attended_ref, slices_ref, weight_ref, slice_sems, sems,
):
    fetched = []
    for count, source in enumerate((slices0_ref, slices1_ref, slices2_ref, slices3_ref)):
        along_x = lax.rem(place_ref[0] + count, MP)
        fetched.append(pltpu.make_async_copy(source, slices_ref.at[:, along_x], slice_sems.at[count]))
        fetched[count].start()
    ready = fetch(gathered_ref, KINDS, weight_ref, sems)
    unpack(pieces_ref, rows_ref)
    normalise(rows_ref, gain_ref[2:3], partner_ref)
    normalise(after_ref, gain_ref[1:2], query_ref)
    queries, partner = query_ref[...], partner_ref[...]
    for copy in fetched:
        copy.wait()

    def query_columns(owner, first, last):
        return slices_ref[owner].reshape(COLS, D)[first:last]

    def quad_of(quad):
        ready(quad)
        return (
            project(queries, query_columns, quad),
            project(partner, of_kind(weight_ref, 0), quad),
            project(partner, of_kind(weight_ref, 1), quad),
        )

    attend(quad_of, attended_ref)
    rows_ref[...] = after_ref[...] + jnp.dot(
        attended_ref[...], out_weight_ref[...], preferred_element_type=jnp.float32
    )
    normalise(rows_ref, gain_ref[3:4], out_ref)


def self_block(pieces, weights, out_weight, gains):
    return pl.pallas_call(
        self_kernel,
        out_shape=jax.ShapeDtypeStruct((TOK, D), jnp.float32),
        in_specs=in_vmem(1) + in_hbm(1) + in_vmem(2),
        out_specs=in_vmem(1)[0],
        scratch_shapes=[pltpu.VMEM((TOK, D), jnp.bfloat16)] * 2
        + [pltpu.VMEM((MP, KINDS, COLS, D), jnp.bfloat16), pltpu.SemaphoreType.DMA((MP,))],
        compiler_params=pltpu.CompilerParams(vmem_limit_bytes=VMEM),
        cost_estimate=estimate(8 * TOK * D * D + 4 * TOK * TOK * D, 8 * 2**20, HEADS * TOK * TOK),
        name="self_block",
    )(pieces, weights, out_weight, gains)


def cross_block(place, after_self, pieces, slices, weights, out_weight, gains):
    kinds = weights.shape[1] - KINDS
    return pl.pallas_call(
        cross_kernel,
        out_shape=jax.ShapeDtypeStruct((TOK, D), jnp.bfloat16),
        in_specs=[pl.BlockSpec(memory_space=pltpu.SMEM)] + in_vmem(2) + in_hbm(MP + 1) + in_vmem(2),
        out_specs=in_vmem(1)[0],
        scratch_shapes=[pltpu.VMEM((TOK, D), jnp.float32)]
        + [pltpu.VMEM((TOK, D), jnp.bfloat16)] * 3
        + [
            pltpu.VMEM((MP,) + slices[0].shape, jnp.bfloat16),
            pltpu.VMEM((MP, kinds, COLS, D), jnp.bfloat16),
            pltpu.SemaphoreType.DMA((MP,)),
            pltpu.SemaphoreType.DMA((MP,)),
        ],
        compiler_params=pltpu.CompilerParams(vmem_limit_bytes=VMEM),
        cost_estimate=estimate(8 * TOK * D * D + 4 * TOK * TOK * D, 8 * 2**20, HEADS * TOK * TOK),
        name="cross_block",
    )(place, after_self, pieces, *slices, weights, out_weight, gains)


def from_mp(value, apart):
    return lax.ppermute(value, "mp", [((index + apart) % MP, index) for index in range(MP)])


def from_x(value, apart):
    count = lax.axis_size("pairs")
    pairs = [(index // MP * MP + (index + apart) % MP, index) for index in range(count)]
    return lax.ppermute(value, "pairs", pairs)


def together_kernel(*refs):
    *sources, out_ref, held_ref, in_sems, out_sems = refs
    arriving = []
    for source in sources:
        for kind in range(source.shape[0]):
            place = len(arriving)
            arriving.append(pltpu.make_async_copy(source.at[kind], held_ref.at[place], in_sems.at[place]))
            arriving[place].start()
    leaving = []
    for place, copy in enumerate(arriving):
        copy.wait()
        leaving.append(pltpu.make_async_copy(held_ref.at[place], out_ref.at[place], out_sems.at[place]))
        leaving[place].start()
    for copy in leaving:
        copy.wait()


def together(*weights):
    count = sum(weight.shape[0] for weight in weights)
    shape = (count,) + weights[0].shape[1:]
    return pl.pallas_call(
        together_kernel,
        out_shape=jax.ShapeDtypeStruct(shape, jnp.bfloat16),
        in_specs=in_hbm(len(weights)),
        out_specs=in_hbm(1)[0],
        scratch_shapes=[
            pltpu.VMEM(shape, jnp.bfloat16),
            pltpu.SemaphoreType.DMA((count,)),
            pltpu.SemaphoreType.DMA((count,)),
        ],
        compiler_params=pltpu.CompilerParams(vmem_limit_bytes=MOST_VMEM),
        cost_estimate=estimate(0, 4 * count * COLS * D),
        name="together",
    )(*weights)


def local(
    enc_tokens,
    pair_views,
    embed_weight,
    self_qkv,
    self_out,
    cross_query,
    cross_kv,
    cross_out,
    norm_gains,
    head_weight,
):
    side_index = lax.axis_index("side")
    flip = [(0, 1), (1, 0)]
    weights = together(*(jnp.swapaxes(weight, 1, 2) for weight in (self_qkv[0], cross_kv[0])))
    weights = lax.all_gather(weights, "mp", axis=0)
    mp_index, x_index = lax.axis_index("mp"), lax.axis_index("pairs") % MP
    quarter = lax.dynamic_slice_in_dim(jnp.swapaxes(cross_query[0], 0, 1), x_index * (COLS // MP), COLS // MP)
    quarters = [quarter] + [from_mp(quarter, apart) for apart in range(1, MP)]
    quarters = jnp.stack([lax.select_n((owner - mp_index) % MP, *quarters) for owner in range(MP)])
    spread = lax.all_to_all(
        embed(enc_tokens, embed_weight, side_index), "pairs", split_axis=0, concat_axis=0, tiled=True
    )
    spread, quarters = lax.optimization_barrier((spread, quarters))
    slices = [quarters] + [from_x(quarters, apart) for apart in range(1, MP)]
    views = enc_tokens.shape[0]
    taken = views // 2
    own = spread.reshape((-1,) + spread.shape[2:])
    other = lax.ppermute(own, "side", flip)
    wanted = jnp.where(side_index == 0, pair_views[:, 0], pair_views[:, 1])
    within = wanted % views
    slots = wanted // views * taken + within % taken
    slots = jnp.where(within // taken == side_index, slots, slots + own.shape[0])
    packets = pick(slots, own, other)
    pieces = lax.all_to_all(packets, ("pairs", "mp"), split_axis=0, concat_axis=0, tiled=True)
    pieces, slices = lax.optimization_barrier((pieces, slices))
    partner = lax.ppermute(pieces, "side", flip)
    after_self = self_block(pieces, weights, self_out[0], norm_gains[0])
    place = x_index.reshape(1)
    final_rows = cross_block(place, after_self, partner, slices, weights, cross_out[0], norm_gains[0])
    final_rows = lax.all_to_all(
        final_rows.reshape(MP, TOK // MP, D), "mp", split_axis=0, concat_axis=0, tiled=True
    )
    result = jnp.einsum("prd,de->pre", final_rows, head_weight[0], preferred_element_type=jnp.float32)
    return result.astype(jnp.bfloat16)[:, None]


def solution(mesh):
    placed = (
        P("pairs", "mp", None),
        P(),
        P(),
        P("side", None, None, "mp"),
        P("side", None, None),
        P("side", None, "mp"),
        P("side", None, None, "mp"),
        P("side", None, None),
        P("side", None, None),
        P("side", None, None),
    )
    return jax.shard_map(
        local, mesh=mesh, in_specs=placed, out_specs=P("pairs", "side", "mp", None), check_vma=False
    )
```
